128 devices in a mesh: outer: 16 (over z_hi, x, core), inner: 8 (over z_lo, y).
Axes of the slice: x: 4, y: 4, z: 4 (z_hi: 2, z_lo: 2; z = z_hi * 2 + z_lo), core: 2. Of those that a mesh axis runs over, the one named last changes fastest.
Arguments:
- queries: bfloat16 [131072, 512], P(('outer', 'inner')), may hold values from -6 to 6
- keys: bfloat16 [131072, 128], P(('outer', 'inner')), may hold values from -6 to 6
- values: bfloat16 [131072, 128], P(('outer', 'inner')), may hold values from -6 to 6
- doc_lengths: int32 [16], replicated, may hold values from 1 to 11264, 131072 in all
Outputs:
- attended: bfloat16 [131072, 512], P(('outer', 'inner'))
The draws below stay inside these ranges and needn't reach their ends.
Inputs may be any that keep to these rules, and one draw needn't show every extreme that they name: `doc_lengths`: 16 lengths in sequence order that sum to 131072, the longest exactly 11264.
All inputs are finite; a program needn't handle non-finite values.
Results may differ from the reference program's by a relative error of at most 0.0065.
Values may be sent and summed in bfloat16 or wider, within the bound.
A program may use at most 832 MiB of HBM per device.

```python
import math
import jax
import jax.numpy as jnp
import numpy as np
from jax import lax

HEAD = 128
QHEADS = 4
TOK_DEV = 1024
REACH = 11
DOC_MOST = 11264
TOKENS = 131072
DOCS = 16


def draw_queries(key, part):
    key = jax.random.fold_in(key, 11)
    first_key, second_key = jax.random.split(key)
    row_scale = jnp.exp(jax.random.uniform(first_key, (TOKENS, 1), minval=math.log(0.5), maxval=math.log(2.0)))
    base = jax.random.normal(second_key, (TOKENS, QHEADS * HEAD), jnp.float32) * row_scale
    return jnp.clip(base, -6.0, 6.0).astype(jnp.bfloat16)


def draw_keys(key, part):
    key = jax.random.fold_in(key, 23)
    base = jax.random.normal(key, (TOKENS, HEAD), jnp.float32)
    return jnp.clip(base, -6.0, 6.0).astype(jnp.bfloat16)


def steps_of(key, shape, cuts, smallest, largest):
    factor_of, own = 1.0, jax.random.fold_in(key, 6)
    for dim, parts in cuts:
        heights = jnp.exp(jax.random.uniform(jax.random.fold_in(own, dim), (parts,), jnp.float32, smallest / len(cuts), largest / len(cuts)))
        factor_of = factor_of * jnp.repeat(heights, shape[dim] // parts).reshape([-1 if axis == dim else 1 for axis in range(len(shape))])
    return factor_of


def profile(number_of, total, limit, slope):
    loads = [(1 << 20) // math.isqrt(rank ** slope) + 1 for rank in range(2, number_of + 1)]
    rest, given = total - limit - (number_of - 1), [1] * (number_of - 1)
    while rest > 0:
        movable = [i for i in range(number_of - 1) if given[i] < limit]
        mass, remaining = sum([loads[i] for i in movable]), rest
        for i in movable:
            addition = min(limit - given[i], max(1, remaining * loads[i] // mass), rest)
            given[i] = given[i] + addition
            rest = rest - addition
    return np.array([limit] + given)


def uneven_parts(key, amount, total, bound, skew):
    if amount == 2:
        one = jax.random.randint(key, (), max(1, total - bound), min(bound, total - 1) + 1)
        return jnp.stack([one, total - one])
    tallies = jnp.asarray(profile(amount, total, bound, skew), jnp.int32)
    couples = (amount - 1) // 2
    giver, sink = tallies[1:1 + 2 * couples:2], tallies[2:2 + 2 * couples:2]
    room = jnp.minimum(giver - 1, bound - sink)
    shifted = jax.random.randint(jax.random.fold_in(key, 1), (couples,), 0, 1 << 20) % (room + 1)
    tallies = tallies.at[1:1 + 2 * couples:2].set(giver - shifted).at[2:2 + 2 * couples:2].set(sink + shifted)
    return tallies[jax.random.permutation(jax.random.fold_in(key, 2), amount)]


def normal_values(rng, dims, scale, most, shards=(), kind=jnp.bfloat16):
    gain = steps_of(rng, dims, shards, -0.22, 0.18) if shards else 1.0
    values = jax.random.normal(rng, dims, jnp.float32) * scale * gain
    return jnp.minimum(jnp.maximum(values, -most), most).astype(kind)


def setup_inputs(seed: int = 0) -> dict:
    key_of = jax.random.split(jax.random.key(seed), 5)
    return {
        "queries": draw_queries(jax.random.fold_in(key_of[4], 71), 0),
        "keys": draw_keys(jax.random.fold_in(key_of[4], 71), 0),
        "values": normal_values(key_of[2], (TOKENS, HEAD), 1.0, 6.0, ((0, 128),)),
        "doc_lengths": uneven_parts(key_of[3], DOCS, TOKENS, DOC_MOST, 2).astype(jnp.int32),
    }


def document(positions, doc_ends):
    return jnp.sum((positions[:, None] >= doc_ends[None, :]).astype(jnp.int32), axis=1)


def reference(queries, keys, values, doc_lengths):
    doc_ends = jnp.cumsum(doc_lengths).astype(jnp.int32)
    span = (REACH + 1) * TOK_DEV
    padding = jnp.zeros((REACH * TOK_DEV, HEAD), keys.dtype)
    padded_keys = jnp.concatenate([padding, keys], axis=0)
    padded_values = jnp.concatenate([padding, values], axis=0)
    blocks = queries.reshape(TOKENS // TOK_DEV, TOK_DEV, QHEADS, HEAD)
    indices = jnp.arange(TOKENS // TOK_DEV, dtype=jnp.int32)

    def one_block(inputs):
        block_index, query_block = inputs
        first_pos = (block_index * TOK_DEV).astype(jnp.int32)
        key_window = lax.dynamic_slice_in_dim(padded_keys, first_pos, span, 0)
        value_window = lax.dynamic_slice_in_dim(padded_values, first_pos, span, 0)
        query_pos = first_pos + jnp.arange(TOK_DEV, dtype=jnp.int32)
        key_pos = first_pos - REACH * TOK_DEV + jnp.arange(span, dtype=jnp.int32)
        visible = (document(query_pos, doc_ends)[:, None] == document(key_pos, doc_ends)[None, :])
        visible = visible & (key_pos[None, :] <= query_pos[:, None]) & (key_pos[None, :] >= 0)
        scores = jnp.einsum("qhd,kd->hqk", query_block.astype(jnp.float32), key_window.astype(jnp.float32))
        scores = scores * (HEAD ** -0.5)
        masked = jnp.where(visible[None], scores, -1e30)
        top = jnp.max(masked, axis=-1)
        weights = jnp.where(visible[None], jnp.exp(masked - top[..., None]), 0.0)
        total = jnp.sum(weights, axis=-1)
        rounded = lax.optimization_barrier(weights.astype(jnp.bfloat16))
        mixed = jnp.einsum("hqk,kd->hqd", rounded.astype(jnp.float32), value_window.astype(jnp.float32))
        output = mixed / total[..., None]
        return jnp.transpose(output, (1, 0, 2)).reshape(TOK_DEV, QHEADS * HEAD).astype(jnp.bfloat16)

    result = lax.map(one_block, (indices, blocks))
    return result.reshape(TOKENS, QHEADS * HEAD)
```

```python
import functools
import jax
import jax.numpy as jnp
from jax import lax
from jax.experimental import pallas as pl
from jax.experimental.pallas import tpu as pltpu
from jax.sharding import PartitionSpec as P

HEAD = 128
QHEADS = 4
REACH = 11
TOK = 1024
GROUP = 8
DOCS = 16
ROWS = 2 * TOK
SCALE = HEAD ** -0.5 * 1.4426950408889634
HIDDEN = -1e30
SAFE = 2.0 ** 100
MESH = pl.DeviceIdType.MESH
CONTRACT_LAST = (((1,), (1,)), ((), ()))


def order_of(c):
    row = c // 4
    beside = [row * 4 + (c + turn) % 4 for turn in (1, 3, 2)]
    across = [(place + 4) % 8 for place in [c] + beside]
    arrival = [c, across[0], beside[0], beside[1], across[1], across[2], beside[2], across[3]]
    before = [place for place in arrival if place >= c - 3]
    others = [8 + place for place in arrival if place < c or place >= c + 5]
    return before + others


def events_of(c):
    across = (c + 4) % 8
    row = c // 4
    beside = [row * 4 + (c + turn) % 4 for turn in (1, 3, 2)]
    second = 1 + sum(place >= c - 3 for place in [across] + beside[:2])
    third = second + sum(place >= c - 3 for place in [(place + 4) % 8 for place in beside[:2]] + beside[2:])
    return second, third


def pick(c, options):
    value = options[0]
    for place in range(1, GROUP):
        value = jnp.where(c == place, options[place], value)
    return value


def edges(lengths_ref):
    lane = lax.broadcasted_iota(jnp.int32, (1, HEAD), 1)
    starts = jnp.zeros((1, HEAD), jnp.int32)
    ends = jnp.zeros((1, HEAD), jnp.int32)
    at = jnp.int32(0)
    for doc in range(DOCS):
        starts = jnp.where(lane == doc, at, starts)
        at = at + lengths_ref[doc]
        ends = jnp.where(lane == doc, at, ends)
    return starts, ends


def inside(block, starts, ends):
    positions = block * TOK + lax.broadcasted_iota(jnp.int32, (TOK, HEAD), 0)
    return (positions >= starts) & (positions < ends)


def with_marks(block, key_rows, starts, ends):
    marks = jnp.where(inside(block, starts, ends), 0.0, HIDDEN).astype(jnp.bfloat16)
    return jnp.concatenate([key_rows, marks], axis=1)


def turned(ref):
    pieces = [ref[TOK + part * HEAD:TOK + (part + 1) * HEAD, :] for part in range(TOK // HEAD)]
    ones = jnp.ones((16, TOK), jnp.bfloat16)
    return jnp.concatenate([jnp.concatenate(pieces, axis=1), ones], axis=0)


def block_at(o, c, slot):
    place = slot % GROUP
    own_group = jnp.where(place < c, o, o - 2)
    return jnp.where(slot < GROUP, o - 1, own_group) * GROUP + place


def kernel(outers, lengths_ref, q_ref, k_ref, v_ref, o_ref, worst_ref, window_ref,
           own, slots, wide, top, acc, send_sem, recv_sem, keep_sem):
    o, c = lax.axis_index("outer"), lax.axis_index("inner")
    row, y = c // 4, c % 4
    c_next, c_prev, c_far = row * 4 + (y + 1) % 4, row * 4 + (y + 3) % 4, row * 4 + (y + 2) % 4
    c_over = (c + 4) % 8
    over_next, over_prev, over_far = (c_next + 4) % 8, (c_prev + 4) % 8, (c_far + 4) % 8
    later, earlier = ((o + 1) % outers, c), ((o + outers - 1) % outers, c)
    at_next, at_prev, at_over = (o, c_next), (o, c_prev), (o, c_over)

    barrier = pltpu.get_barrier_semaphore()
    for device in (later, earlier, at_next, at_prev, at_over):
        pl.semaphore_signal(barrier, inc=1, device_id=device, device_id_type=MESH)
    own[0:TOK, :] = k_ref[...]
    values_t = v_ref[...].T
    for part in range(TOK // HEAD):
        own[TOK + part * HEAD:TOK + (part + 1) * HEAD, :] = values_t[:, part * HEAD:(part + 1) * HEAD]
    pl.semaphore_wait(barrier, 5)

    def copy(source, slot, device, send, part=None):
        if part is None:
            target, recv = slots.at[slot], recv_sem.at[slot]
        else:
            rows = pl.ds(part * TOK, TOK)
            source, target = source.at[rows, :], slots.at[slot, rows, :]
            recv = recv_sem.at[slot if part == 0 else 16]
        return pltpu.make_async_remote_copy(
            src_ref=source, dst_ref=target, send_sem=send_sem.at[send], recv_sem=recv,
            device_id=device, device_id_type=MESH)

    def pass_on(slot, send):
        @pl.when(slot < c)
        def _():
            copy(slots.at[slot], GROUP + slot, earlier, send).start()

        @pl.when(slot >= c + 5)
        def _():
            copy(slots.at[slot], GROUP + slot, later, send).start()

    def passed(slot, send):
        @pl.when((slot < c) | (slot >= c + 5))
        def _():
            copy(slots.at[slot], GROUP + slot, earlier, send).wait_send()

    def arrived(slot, part=None):
        copy(slots.at[slot] if part is None else slots.at[slot], slot, later, 0, part).wait_recv()

    copy(own, c, later, 0).start()

    starts, ends = edges(lengths_ref)
    here = o * GROUP + c
    marks = jnp.where(inside(here, starts, ends), 1.0, 0.0).astype(jnp.bfloat16)
    for head in range(QHEADS):
        wide[head * TOK:(head + 1) * TOK, 0:HEAD] = q_ref[:, head * HEAD:(head + 1) * HEAD]
        wide[head * TOK:(head + 1) * TOK, HEAD:2 * HEAD] = marks

    own_keys = with_marks(here, own[0:TOK, :], starts, ends)
    own_values = turned(own)
    half = TOK // 2
    for head in range(QHEADS):
        for first in (0, half):
            depth = first + half
            at = head * TOK + first
            scores = lax.dot_general(
                own_keys[0:depth], wide[at:at + half, :], CONTRACT_LAST,
                preferred_element_type=jnp.float32)
            key_at = lax.broadcasted_iota(jnp.int32, (depth, half), 0)
            query_at = lax.broadcasted_iota(jnp.int32, (depth, half), 1) + first
            scores = jnp.where(key_at <= query_at, scores * SCALE, HIDDEN)
            highest = jnp.max(scores, axis=0, keepdims=True)
            top[0:1, at:at + half] = highest
            weights = jnp.exp2(scores - highest).astype(jnp.bfloat16)
            acc[:, at:at + half] = jnp.dot(
                own_values[:, 0:depth], weights, preferred_element_type=jnp.float32)

    orders = [order_of(place) for place in range(GROUP)]
    low = pick(c, [sum(slot << (4 * step) for step, slot in enumerate(order[:6])) for order in orders])
    high = pick(c, [sum(slot << (4 * step) for step, slot in enumerate(order[6:])) for order in orders])

    second = pick(c, [events_of(place)[0] for place in range(GROUP)])
    third = pick(c, [events_of(place)[1] for place in range(GROUP)])

    def step_slot(step):
        return jnp.where(
            step < 6,
            lax.shift_right_logical(low, 4 * jnp.minimum(step, 5)) & 15,
            lax.shift_right_logical(high, 4 * jnp.maximum(step - 6, 0)) & 15)

    def work(step, _):
        @pl.when(step == 0)
        def _():
            arrived(c)
            copy(slots.at[c], c, at_next, 1).start()
            copy(slots.at[c], c, at_prev, 2).start()
            copy(slots.at[c], c, at_over, 3).start()

        @pl.when(step == 1)
        def _():
            for slot in (c_over, c_next, c_prev):
                arrived(slot)
            copy(slots.at[c_over], c_over, at_next, 4).start()
            copy(slots.at[c_over], c_over, at_prev, 5).start()
            copy(slots.at[c_prev], c_prev, at_next, 6, 0).start()
            copy(slots.at[c_next], c_next, at_prev, 7, 1).start()
            for send, slot in enumerate((c_over, c_next, c_prev)):
                pass_on(slot, 9 + send)

        @pl.when(step == second)
        def _():
            for slot in (over_next, over_prev):
                arrived(slot)
            arrived(c_far, 0)
            arrived(c_far, 1)
            copy(slots.at[c_far], c_far, at_over, 8).start()
            for send, slot in enumerate((over_next, over_prev, c_far)):
                pass_on(slot, 12 + send)

        @pl.when(step == third)
        def _():
            arrived(over_far)
            pass_on(over_far, 15)

        slot = step_slot(step)

        @pl.when(slot >= GROUP)
        def _():
            arrived(slot)

        pltpu.make_async_copy(slots.at[slot], window_ref.at[step], keep_sem.at[step]).start()
        keys = with_marks(block_at(o, c, slot), slots[slot, 0:TOK, :], starts, ends)
        values = turned(slots.at[slot])
        for head in range(QHEADS):
            columns = slice(head * TOK, (head + 1) * TOK)
            scores = lax.dot_general(
                keys, wide[columns, :], CONTRACT_LAST, preferred_element_type=jnp.float32)
            weights = jnp.exp2(scores * SCALE - top[0:1, columns]).astype(jnp.bfloat16)
            acc[:, columns] += jnp.dot(values, weights, preferred_element_type=jnp.float32)
        return 0

    lax.fori_loop(0, REACH, work, 0)

    worst = jnp.zeros((1, TOK), jnp.float32)
    for head in range(QHEADS):
        columns = slice(head * TOK, (head + 1) * TOK)
        total = acc[HEAD:HEAD + 1, columns]
        worst = jnp.where(total < SAFE, worst, 1.0)
        o_ref[:, head * HEAD:(head + 1) * HEAD] = (acc[0:HEAD, columns] / total).T.astype(jnp.bfloat16)
    worst_ref[...] = jnp.broadcast_to(jnp.max(worst, axis=1, keepdims=True), (8, HEAD))

    copy(own, c, later, 0).wait_send()
    for send, slot, part in ((1, c, None), (2, c, None), (3, c, None), (4, c_over, None),
                             (5, c_over, None), (6, c_prev, 0), (7, c_next, 1), (8, c_far, None)):
        copy(slots.at[slot], slot, at_next, send, part).wait_send()
    for send, slot in enumerate((c_over, c_next, c_prev, over_next, over_prev, c_far, over_far)):
        passed(slot, 9 + send)

    def kept(step, _):
        pltpu.make_async_copy(slots.at[0], window_ref.at[step], keep_sem.at[step]).wait()
        return 0

    lax.fori_loop(0, REACH, kept, 0)


def repair(outer_size, worst_ref, lengths_ref, place_ref, q_hbm, k_hbm, v_hbm, window_hbm, given, out_hbm,
           queries, block_rows, values_t, marks, result, top, acc):
    @pl.when(worst_ref[0, 0] > 0.0)
    def _():
        o, c = place_ref[0], place_ref[1]
        here = o * GROUP + c
        starts, ends = edges(lengths_ref)
        pltpu.sync_copy(q_hbm, queries)
        marks[...] = jnp.where(inside(here, starts, ends), 1.0, 0.0).astype(jnp.bfloat16)
        acc[...] = jnp.zeros_like(acc)
        top[...] = jnp.full_like(top, HIDDEN)

        def scan(keys, head_values, own_block):
            for head in range(QHEADS):
                columns = slice(head * TOK, (head + 1) * TOK)
                wide = jnp.concatenate([queries[:, head * HEAD:(head + 1) * HEAD], marks[...]], axis=1)
                scores = lax.dot_general(keys, wide, CONTRACT_LAST, preferred_element_type=jnp.float32)
                scores = scores * SCALE
                if own_block:
                    key_at = lax.broadcasted_iota(jnp.int32, (TOK, TOK), 0)
                    query_at = lax.broadcasted_iota(jnp.int32, (TOK, TOK), 1)
                    scores = jnp.where(key_at <= query_at, scores, HIDDEN)
                old = top[0:1, columns]
                new = jnp.maximum(old, jnp.max(scores, axis=0, keepdims=True))
                top[0:1, columns] = new
                weights = jnp.exp2(scores - new).astype(jnp.bfloat16)
                acc[:, columns] = acc[:, columns] * jnp.exp2(old - new) + jnp.dot(
                    head_values, weights, preferred_element_type=jnp.float32)

        pltpu.sync_copy(k_hbm, block_rows.at[0:TOK, :])
        pltpu.sync_copy(v_hbm, block_rows.at[TOK:ROWS, :])
        values_t[...] = block_rows[TOK:ROWS, :].T
        ones = jnp.ones((16, TOK), jnp.bfloat16)
        scan(with_marks(here, block_rows[0:TOK, :], starts, ends),
             jnp.concatenate([values_t[...], ones], axis=0), True)

        def one(step, _):
            pltpu.sync_copy(window_hbm.at[step], block_rows)
            block = here - place_ref[2 + step]
            scan(with_marks(block, block_rows[0:TOK, :], starts, ends), turned(block_rows), False)
            return 0

        lax.fori_loop(0, REACH, one, 0)
        for head in range(QHEADS):
            columns = slice(head * TOK, (head + 1) * TOK)
            result[:, head * HEAD:(head + 1) * HEAD] = (
                acc[0:HEAD, columns] / acc[HEAD:HEAD + 1, columns]).T.astype(jnp.bfloat16)
        pltpu.sync_copy(result, out_hbm)


def distances(c):
    return [8 + c - slot if slot < 8 else (c - slot + 8 if slot - 8 < c else 16 + c - (slot - 8))
            for slot in order_of(c)]


def per_device(outers, queries, keys, values, doc_lengths):
    vmem = pl.BlockSpec(memory_space=pltpu.VMEM)
    smem = pl.BlockSpec(memory_space=pltpu.SMEM)
    anywhere = pl.BlockSpec(memory_space=pl.ANY)
    out_shape = jax.ShapeDtypeStruct((TOK, QHEADS * HEAD), jnp.bfloat16)
    first, worst, window = pl.pallas_call(
        functools.partial(kernel, outers),
        out_shape=(out_shape, jax.ShapeDtypeStruct((8, HEAD), jnp.float32),
                   jax.ShapeDtypeStruct((REACH, ROWS, HEAD), jnp.bfloat16)),
        in_specs=[smem, vmem, vmem, vmem],
        out_specs=(vmem, vmem, anywhere),
        scratch_shapes=[
            pltpu.VMEM((ROWS, HEAD), jnp.bfloat16),
            pltpu.VMEM((16, ROWS, HEAD), jnp.bfloat16),
            pltpu.VMEM((QHEADS * TOK, 2 * HEAD), jnp.bfloat16),
            pltpu.VMEM((8, QHEADS * TOK), jnp.float32),
            pltpu.VMEM((HEAD + 16, QHEADS * TOK), jnp.float32),
            pltpu.SemaphoreType.DMA((16,)),
            pltpu.SemaphoreType.DMA((17,)),
            pltpu.SemaphoreType.DMA((REACH,)),
        ],
        compiler_params=pltpu.CompilerParams(
            collective_id=0, has_side_effects=True, vmem_limit_bytes=56 << 20),
        cost_estimate=pl.CostEstimate(
            flops=4 * 12 * QHEADS * TOK * TOK * HEAD, bytes_accessed=12 << 20,
            transcendentals=12 * QHEADS * TOK * TOK),
    )(doc_lengths, queries, keys, values)
    o, c = lax.axis_index("outer"), lax.axis_index("inner")
    table = jnp.array([distances(place) for place in range(GROUP)], jnp.int32)
    place = jnp.concatenate([jnp.stack([o, c]).astype(jnp.int32), table[c]])
    return pl.pallas_call(
        functools.partial(repair, outers),
        out_shape=out_shape,
        in_specs=[smem, smem, smem] + [anywhere] * 5,
        out_specs=anywhere,
        input_output_aliases={7: 0},
        scratch_shapes=[
            pltpu.VMEM((TOK, QHEADS * HEAD), jnp.bfloat16),
            pltpu.VMEM((ROWS, HEAD), jnp.bfloat16),
            pltpu.VMEM((HEAD, TOK), jnp.bfloat16),
            pltpu.VMEM((TOK, HEAD), jnp.bfloat16),
            pltpu.VMEM((TOK, QHEADS * HEAD), jnp.bfloat16),
            pltpu.VMEM((8, QHEADS * TOK), jnp.float32),
            pltpu.VMEM((HEAD + 16, QHEADS * TOK), jnp.float32),
        ],
        compiler_params=pltpu.CompilerParams(vmem_limit_bytes=56 << 20),
    )(worst, doc_lengths, place, queries, keys, values, window, first)


def solution(mesh):
    rows = P(("outer", "inner"), None)
    return jax.shard_map(
        functools.partial(per_device, mesh.shape["outer"]),
        mesh=mesh,
        in_specs=(rows, rows, rows, P()),
        out_specs=rows,
        check_vma=False,
    )
```

```python
import functools
import jax
import jax.numpy as jnp
from jax import lax
from jax.experimental import pallas as pl
from jax.experimental.pallas import tpu as pltpu
from jax.sharding import PartitionSpec as P

HEAD = 128
QHEADS = 4
REACH = 11
TOK = 1024
GROUP = 8
DOCS = 16
ROWS = 2 * TOK
SCALE = HEAD ** -0.5 * 1.4426950408889634
HIDDEN = -1e30
SAFE = 2.0 ** 100
MESH = pl.DeviceIdType.MESH
CONTRACT_LAST = (((1,), (1,)), ((), ()))


SENDS = [
    [606160960, 304096322, 268512322, 415672322, 339879936, 281485708, 667922566, 667871134, 869150852, 659279509, 0, 0, 0, 0, 0],
    [840987714, 136342594, 841053248, 136408128, 436218880, 818295810, 440604311, 440538773, 198109712, 198142084, 898429192, 822700694, 193727291, 2873, 0],
    [610355392, 878733506, 442574016, 272836742, 605103298, 605038724, 411411095, 437280802, 357256985, 931942171, 285781818, 0, 0, 0, 0],
    [845182146, 979374274, 140534978, 440537121, 974154389, 193849610, 881071897, 952623105, 198175512, 444887437, 98470847, 0, 0, 0, 0],
    [614549824, 882993472, 344270146, 609396032, 344207757, 609432898, 294466726, 441590552, 290172860, 437379238, 0, 0, 0, 0, 0],
    [983590210, 849350978, 144733506, 139638024, 898495652, 198108327, 844261774, 902764447, 135303203, 100789148, 100725794, 98470847, 0, 0, 0],
    [618744256, 887185856, 887120322, 281422220, 613785998, 613730336, 298829858, 298723726, 277213086, 277114780, 10771, 0, 0, 0, 0],
    [148927938, 148993472, 144029070, 902804876, 907088168, 907048232, 982868894, 444960935, 436302882, 978479633, 105090181, 0, 0, 0, 0],
    [622938688, 958427714, 320941634, 352858640, 387981840, 357282322, 303112589, 424298663, 609397926, 370177819, 298722206, 23817, 0, 0, 0],
    [857805376, 153185858, 924870208, 319320726, 840012207, 894137244, 907047707, 113697692, 113749124, 109350155, 0, 0, 0, 0, 0],
    [627133120, 895513282, 895578816, 424356502, 622404246, 622340756, 428651156, 320351000, 285815579, 784771337, 420033040, 303081738, 613806640, 18729, 0],
    [157378240, 157312706, 152675988, 898495257, 323708071, 143977240, 911369248, 911412623, 3469, 0, 0, 0, 0, 0, 0],
    [631327552, 899707714, 899773248, 329263896, 294466328, 361581237, 290075418, 348598932, 626730281, 962284081, 957958707, 11562, 0, 0, 0],
    [161507138, 161572672, 156935962, 915731357, 915771823, 152625813, 902787732, 920086198, 844326580, 113675663, 0, 0, 0, 0, 0],
    [635521984, 836856768, 903967680, 971072448, 298791838, 622441372, 630999866, 298725905, 622375442, 957948699, 819342236, 424323998, 966615470, 886530347, 962259372],
    [165680066, 852979119, 152694189, 924324664, 924411308, 122334739, 848629399, 0, 0, 0, 0, 0, 0, 0, 0],
]
COUNTS = [
    [794754, 2921032, 4518732, 5326034, 5326100, 5326100],
    [2654728, 2929354, 4522892, 5850322, 7190168, 7190235],
    [1589508, 3723977, 4785168, 5858578, 5858710, 5858710],
    [1597830, 2658887, 3990283, 5321809, 5858645, 5858710],
    [1327364, 2925127, 4522893, 5326098, 5326100, 5326100],
    [1859974, 3453576, 4527054, 6116627, 6391319, 6391320],
    [1597830, 3723977, 5055503, 5592340, 5592405, 5592405],
    [1327364, 2920966, 4260749, 5317713, 5854549, 5858710],
    [1589508, 3195594, 4522893, 6124883, 6125015, 6125015],
    [1597830, 2392582, 3723978, 4522958, 5325970, 5326100],
    [1597830, 3723977, 5584016, 6657558, 7190234, 7190235],
    [1327364, 2396678, 3195659, 3728268, 4527184, 4527185],
    [1597830, 3990282, 5317712, 6125014, 6125015, 6125015],
    [1327364, 2392583, 3457674, 4523022, 5059730, 5326100],
    [2130440, 4518731, 6382867, 7989018, 7989150, 7989150],
    [532610, 2388356, 2929290, 3461963, 3728269, 3728270],
]
STEPS = [
    [13834480, 13128189, 257471],
    [13843568, 10168773, 250815],
    [5705265, 13397906, 227647],
    [9906737, 6043654, 214014],
    [14326898, 12727679, 216536],
    [5807346, 201223, 214005],
    [6073907, 12930066, 236918],
    [6260403, 9542674, 217206],
    [9264692, 12883383, 241378],
    [6520180, 988571, 241218],
    [13868853, 10631302, 225979],
    [6580021, 14593588, 205051],
    [12008822, 15156010, 245303],
    [2808310, 9883227, 15924],
    [15617975, 6968716, 237101],
    [3002295, 1549622, 237432],
]
OWN = 16
PARTS = 17


def pick(kind, options):
    value = options[0]
    for other in range(1, len(options)):
        value = jnp.where(kind == other, options[other], value)
    return value


def words_for(kind, table):
    return [pick(kind, [words[at] for words in table]) for at in range(len(table[0]))]


def unpack(words, index, per_word, bits):
    word = words[0]
    for at in range(1, len(words)):
        word = jnp.where(index // per_word == at, words[at], word)
    return lax.shift_right_logical(word, bits * (index % per_word)) & ((1 << bits) - 1)


def edges(lengths_ref):
    lane = lax.broadcasted_iota(jnp.int32, (1, HEAD), 1)
    starts = jnp.zeros((1, HEAD), jnp.int32)
    ends = jnp.zeros((1, HEAD), jnp.int32)
    at = jnp.int32(0)
    for doc in range(DOCS):
        starts = jnp.where(lane == doc, at, starts)
        at = at + lengths_ref[doc]
        ends = jnp.where(lane == doc, at, ends)
    return starts, ends


def inside(block, starts, ends):
    positions = block * TOK + lax.broadcasted_iota(jnp.int32, (TOK, HEAD), 0)
    return (positions >= starts) & (positions < ends)


def with_marks(block, key_rows, starts, ends):
    marks = jnp.where(inside(block, starts, ends), 0.0, HIDDEN).astype(jnp.bfloat16)
    return jnp.concatenate([key_rows, marks], axis=1)


def turned(ref):
    pieces = [ref[TOK + part * HEAD:TOK + (part + 1) * HEAD, :] for part in range(TOK // HEAD)]
    ones = jnp.ones((16, TOK), jnp.bfloat16)
    return jnp.concatenate([jnp.concatenate(pieces, axis=1), ones], axis=0)


def block_at(o, c, slot):
    place = slot % GROUP
    own_group = jnp.where(place < c, o, o - 2)
    return jnp.where(slot < GROUP, o - 1, own_group) * GROUP + place


def kernel(outers, lengths_ref, q_ref, k_ref, v_ref, o_ref, worst_ref, window_ref,
           slots, wide, top, acc, send_sem, recv_sem, keep_sem):
    o, c = lax.axis_index("outer"), lax.axis_index("inner")
    core, pair = o % 2, o // 2
    row, y = c // 4, c % 4
    pairs = outers // 2
    after, ahead = (pair + 1) % pairs, (pair + pairs - 1) % pairs
    c_next, c_prev, c_over = row * 4 + (y + 1) % 4, row * 4 + (y + 3) % 4, (c + 4) % 8
    mate = pair * 2 + 1 - core

    barrier = pltpu.get_barrier_semaphore()
    partners = [(mate, c)]
    for there in (0, 1):
        partners += [(after * 2 + there, c), (ahead * 2 + there, c)]
        partners += [(pair * 2 + there, place) for place in (c_next, c_prev, c_over)]
    for device in partners:
        pl.semaphore_signal(barrier, inc=1, device_id=device, device_id_type=MESH)
    slots[OWN, 0:TOK, :] = k_ref[...]
    values_t = v_ref[...].T
    for part in range(TOK // HEAD):
        slots[OWN, TOK + part * HEAD:TOK + (part + 1) * HEAD, :] = values_t[:, part * HEAD:(part + 1) * HEAD]
    kind = c * 2 + core
    sends, counts, steps = (words_for(kind, table) for table in (SENDS, COUNTS, STEPS))
    pl.semaphore_wait(barrier, len(partners))

    def copy(source, target, part, send, device):
        rows = pl.ds(pl.multiple_of(part * TOK, TOK), TOK)
        return pltpu.make_async_remote_copy(
            src_ref=slots.at[source, rows, :], dst_ref=slots.at[target, rows, :],
            send_sem=send_sem.at[send], recv_sem=recv_sem.at[target * 2 + part],
            device_id=device, device_id_type=MESH)

    def send(index, _):
        code = unpack(sends, index, 2, 15)
        waits, part, source, target = code & 1, (code // 2) & 1, (code // 4) & 31, (code // 128) & 15
        way, there = (code // 2048) & 7, code // 16384

        @pl.when(waits == 1)
        def _():
            copy(source, source, part, 0, (mate, c)).wait_recv()

        to_pair = jnp.where(way == 2, after, jnp.where(way == 3, ahead, pair))
        to_place = jnp.where(way == 4, c_next, jnp.where(way == 5, c_prev, jnp.where(way == 6, c_over, c)))
        copy(source, target, part, index, (to_pair * 2 + there, to_place)).start()
        return 0

    def send_upto(turn, done):
        upto = unpack(counts, turn, 4, 6)
        lax.fori_loop(done, upto, send, 0)
        return upto

    done = send_upto(0, 0)

    starts, ends = edges(lengths_ref)
    here = o * GROUP + c
    marks = jnp.where(inside(here, starts, ends), 1.0, 0.0).astype(jnp.bfloat16)
    for head in range(QHEADS):
        wide[head * TOK:(head + 1) * TOK, 0:HEAD] = q_ref[:, head * HEAD:(head + 1) * HEAD]
        wide[head * TOK:(head + 1) * TOK, HEAD:2 * HEAD] = marks

    own_keys = with_marks(here, slots[OWN, 0:TOK, :], starts, ends)
    own_values = turned(slots.at[OWN])
    half = TOK // 2
    for head in range(QHEADS):
        if head == 2:
            done = send_upto(1, done)
        for first in (0, half):
            depth = first + half
            at = head * TOK + first
            scores = lax.dot_general(
                own_keys[0:depth], wide[at:at + half, :], CONTRACT_LAST,
                preferred_element_type=jnp.float32)
            key_at = lax.broadcasted_iota(jnp.int32, (depth, half), 0)
            query_at = lax.broadcasted_iota(jnp.int32, (depth, half), 1) + first
            scores = jnp.where(key_at <= query_at, scores * SCALE, HIDDEN)
            highest = jnp.max(scores, axis=0, keepdims=True)
            top[0:1, at:at + half] = highest
            weights = jnp.exp2(scores - highest).astype(jnp.bfloat16)
            acc[:, at:at + half] = jnp.dot(
                own_values[:, 0:depth], weights, preferred_element_type=jnp.float32)

    def work(step, done):
        done = send_upto(2 + 2 * step, done)
        code = unpack(steps, step, 4, 6)
        slot = code & 15
        for part in (0, 1):
            @pl.when((code // (16 << part)) & 1 == 1)
            def _():
                copy(slot, slot, part, 0, (mate, c)).wait_recv()

        pltpu.make_async_copy(slots.at[slot], window_ref.at[step], keep_sem.at[step]).start()
        keys = with_marks(block_at(o, c, slot), slots[slot, 0:TOK, :], starts, ends)
        values = turned(slots.at[slot])
        for head in range(QHEADS):
            if head == 2:
                done = send_upto(3 + 2 * step, done)
            columns = slice(head * TOK, (head + 1) * TOK)
            scores = lax.dot_general(
                keys, wide[columns, :], CONTRACT_LAST, preferred_element_type=jnp.float32)
            weights = jnp.exp2(scores * SCALE - top[0:1, columns]).astype(jnp.bfloat16)
            acc[:, columns] += jnp.dot(values, weights, preferred_element_type=jnp.float32)
        return done

    done = lax.fori_loop(0, REACH, work, done)

    worst = jnp.zeros((1, TOK), jnp.float32)
    for head in range(QHEADS):
        columns = slice(head * TOK, (head + 1) * TOK)
        total = acc[HEAD:HEAD + 1, columns]
        worst = jnp.where(total < SAFE, worst, 1.0)
        o_ref[:, head * HEAD:(head + 1) * HEAD] = (acc[0:HEAD, columns] / total).T.astype(jnp.bfloat16)
    worst_ref[...] = jnp.broadcast_to(jnp.max(worst, axis=1, keepdims=True), (8, HEAD))

    def sent(index, _):
        copy(OWN, 0, 0, index, (mate, c)).wait_send()
        return 0

    def kept(step, _):
        pltpu.make_async_copy(slots.at[0], window_ref.at[step], keep_sem.at[step]).wait()
        return 0

    lax.fori_loop(0, done, sent, 0)
    lax.fori_loop(0, REACH, kept, 0)


def repair(outer_size, worst_ref, lengths_ref, place_ref, q_hbm, k_hbm, v_hbm, window_hbm, given, out_hbm,
           queries, block_rows, values_t, marks, result, top, acc, pass_sem):
    @pl.when(worst_ref[0, 0] <= 0.0)
    def _():
        chunk = TOK // 4
        parts = [pl.ds(part * chunk, chunk) for part in range(4)]
        reads = [pltpu.make_async_copy(given.at[rows, :], result.at[rows, :], pass_sem.at[0, part])
                 for part, rows in enumerate(parts)]
        writes = [pltpu.make_async_copy(result.at[rows, :], out_hbm.at[rows, :], pass_sem.at[1, part])
                  for part, rows in enumerate(parts)]
        for read in reads:
            read.start()
        for read, write in zip(reads, writes):
            read.wait()
            write.start()
        for write in writes:
            write.wait()

    @pl.when(worst_ref[0, 0] > 0.0)
    def _():
        o, c = place_ref[0], place_ref[1]
        here = o * GROUP + c
        starts, ends = edges(lengths_ref)
        pltpu.sync_copy(q_hbm, queries)
        marks[...] = jnp.where(inside(here, starts, ends), 1.0, 0.0).astype(jnp.bfloat16)
        acc[...] = jnp.zeros_like(acc)
        top[...] = jnp.full_like(top, HIDDEN)

        def scan(keys, head_values, own_block):
            for head in range(QHEADS):
                columns = slice(head * TOK, (head + 1) * TOK)
                wide = jnp.concatenate([queries[:, head * HEAD:(head + 1) * HEAD], marks[...]], axis=1)
                scores = lax.dot_general(keys, wide, CONTRACT_LAST, preferred_element_type=jnp.float32)
                scores = scores * SCALE
                if own_block:
                    key_at = lax.broadcasted_iota(jnp.int32, (TOK, TOK), 0)
                    query_at = lax.broadcasted_iota(jnp.int32, (TOK, TOK), 1)
                    scores = jnp.where(key_at <= query_at, scores, HIDDEN)
                old = top[0:1, columns]
                new = jnp.maximum(old, jnp.max(scores, axis=0, keepdims=True))
                top[0:1, columns] = new
                weights = jnp.exp2(scores - new).astype(jnp.bfloat16)
                acc[:, columns] = acc[:, columns] * jnp.exp2(old - new) + jnp.dot(
                    head_values, weights, preferred_element_type=jnp.float32)

        pltpu.sync_copy(k_hbm, block_rows.at[0:TOK, :])
        pltpu.sync_copy(v_hbm, block_rows.at[TOK:ROWS, :])
        values_t[...] = block_rows[TOK:ROWS, :].T
        ones = jnp.ones((16, TOK), jnp.bfloat16)
        scan(with_marks(here, block_rows[0:TOK, :], starts, ends),
             jnp.concatenate([values_t[...], ones], axis=0), True)

        def one(step, _):
            pltpu.sync_copy(window_hbm.at[step], block_rows)
            block = here - place_ref[2 + step]
            scan(with_marks(block, block_rows[0:TOK, :], starts, ends), turned(block_rows), False)
            return 0

        lax.fori_loop(0, REACH, one, 0)
        for head in range(QHEADS):
            columns = slice(head * TOK, (head + 1) * TOK)
            result[:, head * HEAD:(head + 1) * HEAD] = (
                acc[0:HEAD, columns] / acc[HEAD:HEAD + 1, columns]).T.astype(jnp.bfloat16)
        pltpu.sync_copy(result, out_hbm)


def distances(kind):
    c = kind // 2
    codes = [(STEPS[kind][step // 4] >> (6 * (step % 4))) & 15 for step in range(REACH)]
    return [8 + c - slot if slot < 8 else (c - slot + 8 if slot - 8 < c else 16 + c - (slot - 8))
            for slot in codes]


def per_device(outers, queries, keys, values, doc_lengths):
    vmem = pl.BlockSpec(memory_space=pltpu.VMEM)
    smem = pl.BlockSpec(memory_space=pltpu.SMEM)
    anywhere = pl.BlockSpec(memory_space=pl.ANY)
    out_shape = jax.ShapeDtypeStruct((TOK, QHEADS * HEAD), jnp.bfloat16)
    first, worst, window = pl.pallas_call(
        functools.partial(kernel, outers),
        out_shape=(out_shape, jax.ShapeDtypeStruct((8, HEAD), jnp.float32),
                   jax.ShapeDtypeStruct((REACH, ROWS, HEAD), jnp.bfloat16)),
        in_specs=[smem, vmem, vmem, vmem],
        out_specs=(vmem, vmem, anywhere),
        scratch_shapes=[
            pltpu.VMEM((PARTS, ROWS, HEAD), jnp.bfloat16),
            pltpu.VMEM((QHEADS * TOK, 2 * HEAD), jnp.bfloat16),
            pltpu.VMEM((8, QHEADS * TOK), jnp.float32),
            pltpu.VMEM((HEAD + 16, QHEADS * TOK), jnp.float32),
            pltpu.SemaphoreType.DMA((2 * len(SENDS[0]),)),
            pltpu.SemaphoreType.DMA((2 * OWN,)),
            pltpu.SemaphoreType.DMA((REACH,)),
        ],
        compiler_params=pltpu.CompilerParams(
            collective_id=0, has_side_effects=True, vmem_limit_bytes=56 << 20),
        cost_estimate=pl.CostEstimate(
            flops=4 * 12 * QHEADS * TOK * TOK * HEAD, bytes_accessed=12 << 20,
            transcendentals=12 * QHEADS * TOK * TOK),
    )(doc_lengths, queries, keys, values)
    o, c = lax.axis_index("outer"), lax.axis_index("inner")
    table = jnp.array([distances(kind) for kind in range(2 * GROUP)], jnp.int32)
    place = jnp.concatenate([jnp.stack([o, c]).astype(jnp.int32), table[c * 2 + o % 2]])
    return pl.pallas_call(
        functools.partial(repair, outers),
        out_shape=out_shape,
        in_specs=[smem, smem, smem] + [anywhere] * 5,
        out_specs=anywhere,
        scratch_shapes=[
            pltpu.VMEM((TOK, QHEADS * HEAD), jnp.bfloat16),
            pltpu.VMEM((ROWS, HEAD), jnp.bfloat16),
            pltpu.VMEM((HEAD, TOK), jnp.bfloat16),
            pltpu.VMEM((TOK, HEAD), jnp.bfloat16),
            pltpu.VMEM((TOK, QHEADS * HEAD), jnp.bfloat16),
            pltpu.VMEM((8, QHEADS * TOK), jnp.float32),
            pltpu.VMEM((HEAD + 16, QHEADS * TOK), jnp.float32),
            pltpu.SemaphoreType.DMA((2, 4)),
        ],
        compiler_params=pltpu.CompilerParams(vmem_limit_bytes=56 << 20),
    )(worst, doc_lengths, place, queries, keys, values, window, first)


def solution(mesh):
    rows = P(("outer", "inner"), None)
    return jax.shard_map(
        functools.partial(per_device, mesh.shape["outer"]),
        mesh=mesh,
        in_specs=(rows, rows, rows, P()),
        out_specs=rows,
        check_vma=False,
    )
```

```python
import functools
import jax
import jax.numpy as jnp
from jax import lax
from jax.experimental import pallas as pl
from jax.experimental.pallas import tpu as pltpu
from jax.sharding import PartitionSpec as P

HEAD = 128
QHEADS = 4
REACH = 11
TOK = 1024
GROUP = 8
DOCS = 16
ROWS = 2 * TOK
SCALE = HEAD ** -0.5 * 1.4426950408889634
HIDDEN = -1e30
SAFE = 2.0 ** 100
MESH = pl.DeviceIdType.MESH
CONTRACT_LAST = (((1,), (1,)), ((), ()))


SENDS = [
    [606160960, 304096322, 268512322, 415672322, 339879936, 281485708, 667922566, 667871134, 869150852, 659279509, 0, 0, 0, 0, 0],
    [840987714, 136342594, 841053248, 136408128, 436218880, 818295810, 440604311, 440538773, 198109712, 198142084, 898429192, 822700694, 193727291, 2873, 0],
    [610355392, 878733506, 442574016, 272836742, 605103298, 605038724, 411411095, 437280802, 357256985, 931942171, 285781818, 0, 0, 0, 0],
    [845182146, 979374274, 140534978, 440537121, 974154389, 193849610, 881071897, 952623105, 198175512, 444887437, 98470847, 0, 0, 0, 0],
    [614549824, 882993472, 344270146, 609396032, 344207757, 609432898, 294466726, 441590552, 290172860, 437379238, 0, 0, 0, 0, 0],
    [983590210, 849350978, 144733506, 139638024, 898495652, 198108327, 844261774, 902764447, 135303203, 100789148, 100725794, 98470847, 0, 0, 0],
    [618744256, 887185856, 887120322, 281422220, 613785998, 613730336, 298829858, 298723726, 277213086, 277114780, 10771, 0, 0, 0, 0],
    [148927938, 148993472, 144029070, 902804876, 907088168, 907048232, 982868894, 444960935, 436302882, 978479633, 105090181, 0, 0, 0, 0],
    [622938688, 958427714, 320941634, 352858640, 387981840, 357282322, 303112589, 424298663, 609397926, 370177819, 298722206, 23817, 0, 0, 0],
    [857805376, 153185858, 924870208, 319320726, 840012207, 894137244, 907047707, 113697692, 113749124, 109350155, 0, 0, 0, 0, 0],
    [627133120, 895513282, 895578816, 424356502, 622404246, 622340756, 428651156, 320351000, 285815579, 784771337, 420033040, 303081738, 613806640, 18729, 0],
    [157378240, 157312706, 152675988, 898495257, 323708071, 143977240, 911369248, 911412623, 3469, 0, 0, 0, 0, 0, 0],
    [631327552, 899707714, 899773248, 329263896, 294466328, 361581237, 290075418, 348598932, 626730281, 962284081, 957958707, 11562, 0, 0, 0],
    [161507138, 161572672, 156935962, 915731357, 915771823, 152625813, 902787732, 920086198, 844326580, 113675663, 0, 0, 0, 0, 0],
    [635521984, 836856768, 903967680, 971072448, 298791838, 622441372, 630999866, 298725905, 622375442, 957948699, 819342236, 424323998, 966615470, 886530347, 962259372],
    [165680066, 852979119, 152694189, 924324664, 924411308, 122334739, 848629399, 0, 0, 0, 0, 0, 0, 0, 0],
]
COUNTS = [
    [794754, 2921032, 4518732, 5326034, 5326100, 5326100],
    [2654728, 2929354, 4522892, 5850322, 7190168, 7190235],
    [1589508, 3723977, 4785168, 5858578, 5858710, 5858710],
    [1597830, 2658887, 3990283, 5321809, 5858645, 5858710],
    [1327364, 2925127, 4522893, 5326098, 5326100, 5326100],
    [1859974, 3453576, 4527054, 6116627, 6391319, 6391320],
    [1597830, 3723977, 5055503, 5592340, 5592405, 5592405],
    [1327364, 2920966, 4260749, 5317713, 5854549, 5858710],
    [1589508, 3195594, 4522893, 6124883, 6125015, 6125015],
    [1597830, 2392582, 3723978, 4522958, 5325970, 5326100],
    [1597830, 3723977, 5584016, 6657558, 7190234, 7190235],
    [1327364, 2396678, 3195659, 3728268, 4527184, 4527185],
    [1597830, 3990282, 5317712, 6125014, 6125015, 6125015],
    [1327364, 2392583, 3457674, 4523022, 5059730, 5326100],
    [2130440, 4518731, 6382867, 7989018, 7989150, 7989150],
    [532610, 2388356, 2929290, 3461963, 3728269, 3728270],
]
STEPS = [
    [13834480, 13128189, 257471],
    [13843568, 10168773, 250815],
    [5705265, 13397906, 227647],
    [9906737, 6043654, 214014],
    [14326898, 12727679, 216536],
    [5807346, 201223, 214005],
    [6073907, 12930066, 236918],
    [6260403, 9542674, 217206],
    [9264692, 12883383, 241378],
    [6520180, 988571, 241218],
    [13868853, 10631302, 225979],
    [6580021, 14593588, 205051],
    [12008822, 15156010, 245303],
    [2808310, 9883227, 15924],
    [15617975, 6968716, 237101],
    [3002295, 1549622, 237432],
]
OWN = 16
PARTS = 17


def pick(kind, options):
    value = options[0]
    for other in range(1, len(options)):
        value = jnp.where(kind == other, options[other], value)
    return value


def words_for(kind, table):
    return [pick(kind, [words[at] for words in table]) for at in range(len(table[0]))]


def unpack(words, index, per_word, bits):
    word = words[0]
    for at in range(1, len(words)):
        word = jnp.where(index // per_word == at, words[at], word)
    return lax.shift_right_logical(word, bits * (index % per_word)) & ((1 << bits) - 1)


def edges(lengths_ref):
    lane = lax.broadcasted_iota(jnp.int32, (1, HEAD), 1)
    starts = jnp.zeros((1, HEAD), jnp.int32)
    ends = jnp.zeros((1, HEAD), jnp.int32)
    at = jnp.int32(0)
    for doc in range(DOCS):
        starts = jnp.where(lane == doc, at, starts)
        at = at + lengths_ref[doc]
        ends = jnp.where(lane == doc, at, ends)
    return starts, ends


def inside(block, starts, ends):
    positions = block * TOK + lax.broadcasted_iota(jnp.int32, (TOK, HEAD), 0)
    return (positions >= starts) & (positions < ends)


def with_marks(block, key_rows, starts, ends):
    marks = jnp.where(inside(block, starts, ends), 0.0, HIDDEN).astype(jnp.bfloat16)
    return jnp.concatenate([key_rows, marks], axis=1)


def turned(ref):
    pieces = [ref[TOK + part * HEAD:TOK + (part + 1) * HEAD, :] for part in range(TOK // HEAD)]
    ones = jnp.ones((16, TOK), jnp.bfloat16)
    return jnp.concatenate([jnp.concatenate(pieces, axis=1), ones], axis=0)


def block_at(o, c, slot):
    place = slot % GROUP
    own_group = jnp.where(place < c, o, o - 2)
    return jnp.where(slot < GROUP, o - 1, own_group) * GROUP + place


def kernel(outers, lengths_ref, q_ref, k_ref, v_ref, o_ref, worst_ref, window_ref,
           slots, wide, top, acc, send_sem, recv_sem, keep_sem):
    o, c = lax.axis_index("outer"), lax.axis_index("inner")
    core, pair = o % 2, o // 2
    row, y = c // 4, c % 4
    pairs = outers // 2
    after, ahead = (pair + 1) % pairs, (pair + pairs - 1) % pairs
    c_next, c_prev, c_over = row * 4 + (y + 1) % 4, row * 4 + (y + 3) % 4, (c + 4) % 8
    mate = pair * 2 + 1 - core

    barrier = pltpu.get_barrier_semaphore()
    partners = [(mate, c)]
    for there in (0, 1):
        partners += [(after * 2 + there, c), (ahead * 2 + there, c)]
        partners += [(pair * 2 + there, place) for place in (c_next, c_prev, c_over)]
    for device in partners:
        pl.semaphore_signal(barrier, inc=1, device_id=device, device_id_type=MESH)
    slots[OWN, 0:TOK, :] = k_ref[...]
    values_t = v_ref[...].T
    for part in range(TOK // HEAD):
        slots[OWN, TOK + part * HEAD:TOK + (part + 1) * HEAD, :] = values_t[:, part * HEAD:(part + 1) * HEAD]
    kind = c * 2 + core
    sends, counts, steps = (words_for(kind, table) for table in (SENDS, COUNTS, STEPS))
    pl.semaphore_wait(barrier, len(partners))

    def copy(source, target, part, send, device):
        rows = pl.ds(pl.multiple_of(part * TOK, TOK), TOK)
        return pltpu.make_async_remote_copy(
            src_ref=slots.at[source, rows, :], dst_ref=slots.at[target, rows, :],
            send_sem=send_sem.at[send], recv_sem=recv_sem.at[target * 2 + part],
            device_id=device, device_id_type=MESH)

    def send(index, _):
        code = unpack(sends, index, 2, 15)
        waits, part, source, target = code & 1, (code // 2) & 1, (code // 4) & 31, (code // 128) & 15
        way, there = (code // 2048) & 7, code // 16384

        @pl.when(waits == 1)
        def _():
            copy(source, source, part, 0, (mate, c)).wait_recv()

        to_pair = jnp.where(way == 2, after, jnp.where(way == 3, ahead, pair))
        to_place = jnp.where(way == 4, c_next, jnp.where(way == 5, c_prev, jnp.where(way == 6, c_over, c)))
        copy(source, target, part, index, (to_pair * 2 + there, to_place)).start()
        return 0

    def send_upto(turn, done):
        upto = unpack(counts, turn, 4, 6)
        lax.fori_loop(done, upto, send, 0)
        return upto

    done = send_upto(0, 0)

    starts, ends = edges(lengths_ref)
    here = o * GROUP + c
    marks = jnp.where(inside(here, starts, ends), 1.0, 0.0).astype(jnp.bfloat16)
    for head in range(QHEADS):
        wide[head * TOK:(head + 1) * TOK, 0:HEAD] = q_ref[:, head * HEAD:(head + 1) * HEAD]
        wide[head * TOK:(head + 1) * TOK, HEAD:2 * HEAD] = marks

    own_keys = with_marks(here, slots[OWN, 0:TOK, :], starts, ends)
    own_values = turned(slots.at[OWN])
    half = TOK // 2
    for head in range(QHEADS):
        if head == 2:
            done = send_upto(1, done)
        for first in (0, half):
            depth = first + half
            at = head * TOK + first
            scores = lax.dot_general(
                own_keys[0:depth], wide[at:at + half, :], CONTRACT_LAST,
                preferred_element_type=jnp.float32)
            key_at = lax.broadcasted_iota(jnp.int32, (depth, half), 0)
            query_at = lax.broadcasted_iota(jnp.int32, (depth, half), 1) + first
            scores = jnp.where(key_at <= query_at, scores * SCALE, HIDDEN)
            highest = jnp.max(scores, axis=0, keepdims=True)
            top[0:1, at:at + half] = highest
            weights = jnp.exp2(scores - highest).astype(jnp.bfloat16)
            acc[:, at:at + half] = jnp.dot(
                own_values[:, 0:depth], weights, preferred_element_type=jnp.float32)

    def work(step, done):
        done = send_upto(2 + 2 * step, done)
        code = unpack(steps, step, 4, 6)
        slot = code & 15
        for part in (0, 1):
            @pl.when((code // (16 << part)) & 1 == 1)
            def _():
                copy(slot, slot, part, 0, (mate, c)).wait_recv()

        pltpu.make_async_copy(slots.at[slot], window_ref.at[step], keep_sem.at[step]).start()
        keys = with_marks(block_at(o, c, slot), slots[slot, 0:TOK, :], starts, ends)
        values = turned(slots.at[slot])
        for head in range(QHEADS):
            if head == 2:
                done = send_upto(3 + 2 * step, done)
            columns = slice(head * TOK, (head + 1) * TOK)
            scores = lax.dot_general(
                keys, wide[columns, :], CONTRACT_LAST, preferred_element_type=jnp.float32)
            weights = jnp.exp2(scores * SCALE - top[0:1, columns]).astype(jnp.bfloat16)
            acc[:, columns] += jnp.dot(values, weights, preferred_element_type=jnp.float32)
        return done

    done = lax.fori_loop(0, REACH, work, done)

    worst = jnp.zeros((1, TOK), jnp.float32)
    for head in range(QHEADS):
        columns = slice(head * TOK, (head + 1) * TOK)
        total = acc[HEAD:HEAD + 1, columns]
        worst = jnp.where(total < SAFE, worst, 1.0)
        o_ref[:, head * HEAD:(head + 1) * HEAD] = (acc[0:HEAD, columns] / total).T.astype(jnp.bfloat16)
    worst_ref[...] = jnp.broadcast_to(jnp.max(worst, axis=1, keepdims=True), (8, HEAD))

    def sent(index, _):
        copy(OWN, 0, 0, index, (mate, c)).wait_send()
        return 0

    def kept(step, _):
        pltpu.make_async_copy(slots.at[0], window_ref.at[step], keep_sem.at[step]).wait()
        return 0

    lax.fori_loop(0, done, sent, 0)
    lax.fori_loop(0, REACH, kept, 0)


def repair(worst_ref, lengths_ref, q_hbm, k_hbm, v_hbm, window_hbm, given, out_hbm,
           queries, block_rows, values_t, marks, result, top, acc, pass_sem):
    @pl.when(worst_ref[0, 0] <= 0.0)
    def _():
        chunk = TOK // 4
        parts = [pl.ds(part * chunk, chunk) for part in range(4)]
        reads = [pltpu.make_async_copy(given.at[rows, :], result.at[rows, :], pass_sem.at[0, part])
                 for part, rows in enumerate(parts)]
        writes = [pltpu.make_async_copy(result.at[rows, :], out_hbm.at[rows, :], pass_sem.at[1, part])
                  for part, rows in enumerate(parts)]
        for read in reads:
            read.start()
        for read, write in zip(reads, writes):
            read.wait()
            write.start()
        for write in writes:
            write.wait()

    @pl.when(worst_ref[0, 0] > 0.0)
    def _():
        o, c = lax.axis_index("outer"), lax.axis_index("inner")
        here = o * GROUP + c
        steps = words_for(c * 2 + o % 2, STEPS)
        starts, ends = edges(lengths_ref)
        pltpu.sync_copy(q_hbm, queries)
        marks[...] = jnp.where(inside(here, starts, ends), 1.0, 0.0).astype(jnp.bfloat16)
        acc[...] = jnp.zeros_like(acc)
        top[...] = jnp.full_like(top, HIDDEN)

        def scan(keys, head_values, own_block):
            for head in range(QHEADS):
                columns = slice(head * TOK, (head + 1) * TOK)
                wide = jnp.concatenate([queries[:, head * HEAD:(head + 1) * HEAD], marks[...]], axis=1)
                scores = lax.dot_general(keys, wide, CONTRACT_LAST, preferred_element_type=jnp.float32)
                scores = scores * SCALE
                if own_block:
                    key_at = lax.broadcasted_iota(jnp.int32, (TOK, TOK), 0)
                    query_at = lax.broadcasted_iota(jnp.int32, (TOK, TOK), 1)
                    scores = jnp.where(key_at <= query_at, scores, HIDDEN)
                old = top[0:1, columns]
                new = jnp.maximum(old, jnp.max(scores, axis=0, keepdims=True))
                top[0:1, columns] = new
                weights = jnp.exp2(scores - new).astype(jnp.bfloat16)
                acc[:, columns] = acc[:, columns] * jnp.exp2(old - new) + jnp.dot(
                    head_values, weights, preferred_element_type=jnp.float32)

        pltpu.sync_copy(k_hbm, block_rows.at[0:TOK, :])
        pltpu.sync_copy(v_hbm, block_rows.at[TOK:ROWS, :])
        values_t[...] = block_rows[TOK:ROWS, :].T
        ones = jnp.ones((16, TOK), jnp.bfloat16)
        scan(with_marks(here, block_rows[0:TOK, :], starts, ends),
             jnp.concatenate([values_t[...], ones], axis=0), True)

        def one(step, _):
            pltpu.sync_copy(window_hbm.at[step], block_rows)
            block = block_at(o, c, unpack(steps, step, 4, 6) & 15)
            scan(with_marks(block, block_rows[0:TOK, :], starts, ends), turned(block_rows), False)
            return 0

        lax.fori_loop(0, REACH, one, 0)
        for head in range(QHEADS):
            columns = slice(head * TOK, (head + 1) * TOK)
            result[:, head * HEAD:(head + 1) * HEAD] = (
                acc[0:HEAD, columns] / acc[HEAD:HEAD + 1, columns]).T.astype(jnp.bfloat16)
        pltpu.sync_copy(result, out_hbm)


def per_device(outers, queries, keys, values, doc_lengths):
    vmem = pl.BlockSpec(memory_space=pltpu.VMEM)
    smem = pl.BlockSpec(memory_space=pltpu.SMEM)
    anywhere = pl.BlockSpec(memory_space=pl.ANY)
    out_shape = jax.ShapeDtypeStruct((TOK, QHEADS * HEAD), jnp.bfloat16)
    first, worst, window = pl.pallas_call(
        functools.partial(kernel, outers),
        out_shape=(out_shape, jax.ShapeDtypeStruct((8, HEAD), jnp.float32),
                   jax.ShapeDtypeStruct((REACH, ROWS, HEAD), jnp.bfloat16)),
        in_specs=[smem, vmem, vmem, vmem],
        out_specs=(vmem, vmem, anywhere),
        scratch_shapes=[
            pltpu.VMEM((PARTS, ROWS, HEAD), jnp.bfloat16),
            pltpu.VMEM((QHEADS * TOK, 2 * HEAD), jnp.bfloat16),
            pltpu.VMEM((8, QHEADS * TOK), jnp.float32),
            pltpu.VMEM((HEAD + 16, QHEADS * TOK), jnp.float32),
            pltpu.SemaphoreType.DMA((2 * len(SENDS[0]),)),
            pltpu.SemaphoreType.DMA((2 * OWN,)),
            pltpu.SemaphoreType.DMA((REACH,)),
        ],
        compiler_params=pltpu.CompilerParams(
            collective_id=0, has_side_effects=True, vmem_limit_bytes=56 << 20),
        cost_estimate=pl.CostEstimate(
            flops=4 * 12 * QHEADS * TOK * TOK * HEAD, bytes_accessed=12 << 20,
            transcendentals=12 * QHEADS * TOK * TOK),
    )(doc_lengths, queries, keys, values)
    return pl.pallas_call(
        repair,
        out_shape=out_shape,
        in_specs=[smem, smem] + [anywhere] * 5,
        out_specs=anywhere,
        scratch_shapes=[
            pltpu.VMEM((TOK, QHEADS * HEAD), jnp.bfloat16),
            pltpu.VMEM((ROWS, HEAD), jnp.bfloat16),
            pltpu.VMEM((HEAD, TOK), jnp.bfloat16),
            pltpu.VMEM((TOK, HEAD), jnp.bfloat16),
            pltpu.VMEM((TOK, QHEADS * HEAD), jnp.bfloat16),
            pltpu.VMEM((8, QHEADS * TOK), jnp.float32),
            pltpu.VMEM((HEAD + 16, QHEADS * TOK), jnp.float32),
            pltpu.SemaphoreType.DMA((2, 4)),
        ],
        compiler_params=pltpu.CompilerParams(vmem_limit_bytes=56 << 20),
    )(worst, doc_lengths, queries, keys, values, window, first)


def solution(mesh):
    rows = P(("outer", "inner"), None)
    return jax.shard_map(
        functools.partial(per_device, mesh.shape["outer"]),
        mesh=mesh,
        in_specs=(rows, rows, rows, P()),
        out_specs=rows,
        check_vma=False,
    )
```

```python
import functools
import jax
import jax.numpy as jnp
from jax import lax
from jax.experimental import pallas as pl
from jax.experimental.pallas import tpu as pltpu
from jax.sharding import PartitionSpec as P

HEAD = 128
QHEADS = 4
REACH = 11
TOK = 1024
GROUP = 8
DOCS = 16
ROWS = 2 * TOK
SCALE = HEAD ** -0.5 * 1.4426950408889634
HIDDEN = -1e30
SAFE = 2.0 ** 100
MESH = pl.DeviceIdType.MESH
CONTRACT_LAST = (((1,), (1,)), ((), ()))


SENDS = [
    [606160960, 304100416, 438380546, 335552514, 281424268, 285815049, 667918734, 667824262, 352921533, 663595536, 0, 0, 0, 0],
    [136408128, 975266880, 136342594, 975201346, 302066690, 872428940, 189437853, 889743492, 198144398, 894132752, 189467319, 94145204, 13579, 0],
    [610355392, 878799040, 339879106, 442572932, 605037760, 605104393, 927705222, 290136064, 927642656, 806367629, 396111674, 0, 0, 0],
    [140534978, 845182146, 979374274, 135312516, 974154389, 827027722, 193763099, 881094920, 198173728, 898462092, 98492947, 98536251, 2873, 0],
    [614549824, 882993472, 344208706, 609461570, 415672586, 294504612, 441590552, 290170022, 931950362, 0, 0, 0, 0, 0],
    [144733506, 983590208, 849416514, 139699464, 898397350, 844313864, 885482661, 902797213, 978456611, 198142348, 98560924, 98496910, 100790668, 3073],
    [618744256, 820013506, 820079040, 281425346, 281487756, 613697571, 348604714, 936321950, 445915403, 873557916, 294499626, 18599, 0, 0],
    [987828672, 987763138, 982880553, 144010142, 907113505, 449209246, 139703299, 814025729, 139594885, 831304836, 982805009, 0, 0, 0],
    [622938688, 958493248, 419964482, 420028944, 357278621, 432949677, 303115296, 780465945, 613796137, 0, 0, 0, 0, 0],
    [857805376, 153185856, 924935744, 907128336, 319320988, 961228306, 894046639, 835588261, 911348011, 839978119, 373493134, 105046414, 0, 0],
    [627133120, 962620098, 962685632, 357246658, 290140822, 622438080, 361540244, 424288786, 285755953, 419981478, 1003398310, 1003481252, 303160717, 0],
    [157378240, 157312706, 965546547, 144043173, 143979027, 109438514, 109374234, 839969958, 113741197, 0, 0, 0, 0, 0],
    [631327552, 899773248, 899707714, 428616472, 294463298, 428690103, 424288916, 361581237, 365949620, 348598803, 12817, 0, 0, 0],
    [866194240, 866128706, 156935960, 915796892, 915706287, 844360606, 861627031, 920063505, 113741331, 3469, 0, 0, 0, 0],
    [635521984, 971074496, 903963586, 836793280, 432939932, 630993822, 631065137, 966536094, 365840947, 890774299, 298802837, 311749170, 370193044, 0],
    [165745600, 920097329, 920020398, 852890163, 161279536, 965600555, 956949273, 961154709, 907087511, 0, 0, 0, 0, 0],
]
COUNTS = [
    [1056898, 3187336, 4256653, 5326034, 5326100, 5326100],
    [2392584, 2929289, 4518732, 6382866, 6657625, 6657625],
    [1327364, 3461833, 5055567, 5592339, 5858710, 5858710],
    [1859974, 2662984, 3994444, 5317711, 6387093, 6657625],
    [1327364, 2662983, 3990348, 4793423, 4793490, 4793490],
    [1859974, 3195528, 4789198, 6649172, 7190169, 7190235],
    [1859974, 3990282, 5584017, 6124950, 6125015, 6125015],
    [1065220, 2920901, 3728140, 5317776, 5858710, 5858710],
    [1327364, 2662919, 4260684, 4523024, 4793490, 4793490],
    [1859974, 2929223, 4256588, 5850257, 6391319, 6391320],
    [1859974, 4256587, 5850322, 6923799, 6923930, 6923930],
    [1065220, 1864133, 2925063, 4252557, 4789264, 4793490],
    [1597830, 3728138, 5321808, 5592405, 5592405, 5592405],
    [1327364, 2654726, 3457739, 4252557, 5055632, 5059795],
    [2130440, 4256587, 5850258, 6919767, 6923930, 6923930],
    [532610, 2388356, 3461835, 4785166, 4793490, 4793490],
]
STEPS = [
    [13061360, 14088343, 257878],
    [13835504, 16636263, 191890],
    [9113137, 13778821, 224767],
    [10640561, 5454854, 58327],
    [5872754, 16604195, 232759],
    [2571698, 4152391, 213016],
    [4947635, 12936752, 216409],
    [2788851, 9963122, 138596],
    [13458996, 10426534, 44651],
    [6512116, 7040219, 207425],
    [3382581, 2075814, 243928],
    [7511477, 14427402, 241896],
    [3648886, 15036723, 245308],
    [2809334, 15832411, 15876],
    [3362743, 10641110, 237418],
    [12109559, 1393080, 110205],
]
OWN = 16
PARTS = 17


def pick(kind, options):
    value = options[0]
    for other in range(1, len(options)):
        value = jnp.where(kind == other, options[other], value)
    return value


def words_for(kind, table):
    return [pick(kind, [words[at] for words in table]) for at in range(len(table[0]))]


def unpack(words, index, per_word, bits):
    word = words[0]
    for at in range(1, len(words)):
        word = jnp.where(index // per_word == at, words[at], word)
    return lax.shift_right_logical(word, bits * (index % per_word)) & ((1 << bits) - 1)


def edges(lengths_ref):
    lane = lax.broadcasted_iota(jnp.int32, (1, HEAD), 1)
    starts = jnp.zeros((1, HEAD), jnp.int32)
    ends = jnp.zeros((1, HEAD), jnp.int32)
    at = jnp.int32(0)
    for doc in range(DOCS):
        starts = jnp.where(lane == doc, at, starts)
        at = at + lengths_ref[doc]
        ends = jnp.where(lane == doc, at, ends)
    return starts, ends


def inside(block, starts, ends):
    positions = block * TOK + lax.broadcasted_iota(jnp.int32, (TOK, HEAD), 0)
    return (positions >= starts) & (positions < ends)


def with_marks(block, key_rows, starts, ends):
    marks = jnp.where(inside(block, starts, ends), 0.0, HIDDEN).astype(jnp.bfloat16)
    return jnp.concatenate([key_rows, marks], axis=1)


def turned(ref):
    pieces = [ref[TOK + part * HEAD:TOK + (part + 1) * HEAD, :] for part in range(TOK // HEAD)]
    ones = jnp.ones((16, TOK), jnp.bfloat16)
    return jnp.concatenate([jnp.concatenate(pieces, axis=1), ones], axis=0)


def block_at(o, c, slot):
    place = slot % GROUP
    own_group = jnp.where(place < c, o, o - 2)
    return jnp.where(slot < GROUP, o - 1, own_group) * GROUP + place


def kernel(outers, lengths_ref, q_ref, k_ref, v_ref, o_ref, worst_ref, window_ref,
           slots, wide, top, acc, send_sem, recv_sem, keep_sem):
    o, c = lax.axis_index("outer"), lax.axis_index("inner")
    core, pair = o % 2, o // 2
    row, y = c // 4, c % 4
    pairs = outers // 2
    after, ahead = (pair + 1) % pairs, (pair + pairs - 1) % pairs
    c_next, c_prev, c_over = row * 4 + (y + 1) % 4, row * 4 + (y + 3) % 4, (c + 4) % 8
    mate = pair * 2 + 1 - core

    barrier = pltpu.get_barrier_semaphore()
    partners = [(mate, c)]
    for there in (0, 1):
        partners += [(after * 2 + there, c), (ahead * 2 + there, c)]
        partners += [(pair * 2 + there, place) for place in (c_next, c_prev, c_over)]
    for device in partners:
        pl.semaphore_signal(barrier, inc=1, device_id=device, device_id_type=MESH)
    slots[OWN, 0:TOK, :] = k_ref[...]
    values_t = v_ref[...].T
    for part in range(TOK // HEAD):
        slots[OWN, TOK + part * HEAD:TOK + (part + 1) * HEAD, :] = values_t[:, part * HEAD:(part + 1) * HEAD]
    kind = c * 2 + core
    sends, counts, steps = (words_for(kind, table) for table in (SENDS, COUNTS, STEPS))
    pl.semaphore_wait(barrier, len(partners))

    def copy(source, target, part, send, device):
        rows = pl.ds(pl.multiple_of(part * TOK, TOK), TOK)
        return pltpu.make_async_remote_copy(
            src_ref=slots.at[source, rows, :], dst_ref=slots.at[target, rows, :],
            send_sem=send_sem.at[send], recv_sem=recv_sem.at[target * 2 + part],
            device_id=device, device_id_type=MESH)

    def send(index, _):
        code = unpack(sends, index, 2, 15)
        waits, part, source, target = code & 1, (code // 2) & 1, (code // 4) & 31, (code // 128) & 15
        way, there = (code // 2048) & 7, code // 16384

        @pl.when(waits == 1)
        def _():
            copy(source, source, part, 0, (mate, c)).wait_recv()

        to_pair = jnp.where(way == 2, after, jnp.where(way == 3, ahead, pair))
        to_place = jnp.where(way == 4, c_next, jnp.where(way == 5, c_prev, jnp.where(way == 6, c_over, c)))
        copy(source, target, part, index, (to_pair * 2 + there, to_place)).start()
        return 0

    def send_upto(turn, done):
        upto = unpack(counts, turn, 4, 6)
        lax.fori_loop(done, upto, send, 0)
        return upto

    done = send_upto(0, 0)

    starts, ends = edges(lengths_ref)
    here = o * GROUP + c
    marks = jnp.where(inside(here, starts, ends), 1.0, 0.0).astype(jnp.bfloat16)
    for head in range(QHEADS):
        wide[head * TOK:(head + 1) * TOK, 0:HEAD] = q_ref[:, head * HEAD:(head + 1) * HEAD]
        wide[head * TOK:(head + 1) * TOK, HEAD:2 * HEAD] = marks

    own_keys = with_marks(here, slots[OWN, 0:TOK, :], starts, ends)
    own_values = turned(slots.at[OWN])
    half = TOK // 2
    for head in range(QHEADS):
        if head == 2:
            done = send_upto(1, done)
        for first in (0, half):
            depth = first + half
            at = head * TOK + first
            scores = lax.dot_general(
                own_keys[0:depth], wide[at:at + half, :], CONTRACT_LAST,
                preferred_element_type=jnp.float32)
            key_at = lax.broadcasted_iota(jnp.int32, (depth, half), 0)
            query_at = lax.broadcasted_iota(jnp.int32, (depth, half), 1) + first
            scores = jnp.where(key_at <= query_at, scores * SCALE, HIDDEN)
            highest = jnp.max(scores, axis=0, keepdims=True)
            top[0:1, at:at + half] = highest
            weights = jnp.exp2(scores - highest).astype(jnp.bfloat16)
            acc[:, at:at + half] = jnp.dot(
                own_values[:, 0:depth], weights, preferred_element_type=jnp.float32)

    def work(step, done):
        done = send_upto(2 + 2 * step, done)
        code = unpack(steps, step, 4, 6)
        slot = code & 15
        for part in (0, 1):
            @pl.when((code // (16 << part)) & 1 == 1)
            def _():
                copy(slot, slot, part, 0, (mate, c)).wait_recv()

        pltpu.make_async_copy(slots.at[slot], window_ref.at[step], keep_sem.at[step]).start()
        keys = with_marks(block_at(o, c, slot), slots[slot, 0:TOK, :], starts, ends)
        values = turned(slots.at[slot])
        for head in range(QHEADS):
            if head == 2:
                done = send_upto(3 + 2 * step, done)
            columns = slice(head * TOK, (head + 1) * TOK)
            scores = lax.dot_general(
                keys, wide[columns, :], CONTRACT_LAST, preferred_element_type=jnp.float32)
            weights = jnp.exp2(scores * SCALE - top[0:1, columns]).astype(jnp.bfloat16)
            acc[:, columns] += jnp.dot(values, weights, preferred_element_type=jnp.float32)
        return done

    done = lax.fori_loop(0, REACH, work, done)

    worst = jnp.zeros((1, TOK), jnp.float32)
    for head in range(QHEADS):
        columns = slice(head * TOK, (head + 1) * TOK)
        total = acc[HEAD:HEAD + 1, columns]
        worst = jnp.where(total < SAFE, worst, 1.0)
        o_ref[:, head * HEAD:(head + 1) * HEAD] = (acc[0:HEAD, columns] / total).T.astype(jnp.bfloat16)
    worst_ref[...] = jnp.broadcast_to(jnp.max(worst, axis=1, keepdims=True), (8, HEAD))

    def sent(index, _):
        copy(OWN, 0, 0, index, (mate, c)).wait_send()
        return 0

    def kept(step, _):
        pltpu.make_async_copy(slots.at[0], window_ref.at[step], keep_sem.at[step]).wait()
        return 0

    lax.fori_loop(0, done, sent, 0)
    lax.fori_loop(0, REACH, kept, 0)


def repair(worst_ref, lengths_ref, q_hbm, k_hbm, v_hbm, window_hbm, given, out_hbm,
           queries, block_rows, values_t, marks, result, top, acc, pass_sem):
    @pl.when(worst_ref[0, 0] <= 0.0)
    def _():
        chunk = TOK // 4
        parts = [pl.ds(part * chunk, chunk) for part in range(4)]
        reads = [pltpu.make_async_copy(given.at[rows, :], result.at[rows, :], pass_sem.at[0, part])
                 for part, rows in enumerate(parts)]
        writes = [pltpu.make_async_copy(result.at[rows, :], out_hbm.at[rows, :], pass_sem.at[1, part])
                  for part, rows in enumerate(parts)]
        for read in reads:
            read.start()
        for read, write in zip(reads, writes):
            read.wait()
            write.start()
        for write in writes:
            write.wait()

    @pl.when(worst_ref[0, 0] > 0.0)
    def _():
        o, c = lax.axis_index("outer"), lax.axis_index("inner")
        here = o * GROUP + c
        steps = words_for(c * 2 + o % 2, STEPS)
        starts, ends = edges(lengths_ref)
        pltpu.sync_copy(q_hbm, queries)
        marks[...] = jnp.where(inside(here, starts, ends), 1.0, 0.0).astype(jnp.bfloat16)
        acc[...] = jnp.zeros_like(acc)
        top[...] = jnp.full_like(top, HIDDEN)

        def scan(keys, head_values, own_block):
            for head in range(QHEADS):
                columns = slice(head * TOK, (head + 1) * TOK)
                wide = jnp.concatenate([queries[:, head * HEAD:(head + 1) * HEAD], marks[...]], axis=1)
                scores = lax.dot_general(keys, wide, CONTRACT_LAST, preferred_element_type=jnp.float32)
                scores = scores * SCALE
                if own_block:
                    key_at = lax.broadcasted_iota(jnp.int32, (TOK, TOK), 0)
                    query_at = lax.broadcasted_iota(jnp.int32, (TOK, TOK), 1)
                    scores = jnp.where(key_at <= query_at, scores, HIDDEN)
                old = top[0:1, columns]
                new = jnp.maximum(old, jnp.max(scores, axis=0, keepdims=True))
                top[0:1, columns] = new
                weights = jnp.exp2(scores - new).astype(jnp.bfloat16)
                acc[:, columns] = acc[:, columns] * jnp.exp2(old - new) + jnp.dot(
                    head_values, weights, preferred_element_type=jnp.float32)

        pltpu.sync_copy(k_hbm, block_rows.at[0:TOK, :])
        pltpu.sync_copy(v_hbm, block_rows.at[TOK:ROWS, :])
        values_t[...] = block_rows[TOK:ROWS, :].T
        ones = jnp.ones((16, TOK), jnp.bfloat16)
        scan(with_marks(here, block_rows[0:TOK, :], starts, ends),
             jnp.concatenate([values_t[...], ones], axis=0), True)

        def one(step, _):
            pltpu.sync_copy(window_hbm.at[step], block_rows)
            block = block_at(o, c, unpack(steps, step, 4, 6) & 15)
            scan(with_marks(block, block_rows[0:TOK, :], starts, ends), turned(block_rows), False)
            return 0

        lax.fori_loop(0, REACH, one, 0)
        for head in range(QHEADS):
            columns = slice(head * TOK, (head + 1) * TOK)
            result[:, head * HEAD:(head + 1) * HEAD] = (
                acc[0:HEAD, columns] / acc[HEAD:HEAD + 1, columns]).T.astype(jnp.bfloat16)
        pltpu.sync_copy(result, out_hbm)


def per_device(outers, queries, keys, values, doc_lengths):
    vmem = pl.BlockSpec(memory_space=pltpu.VMEM)
    smem = pl.BlockSpec(memory_space=pltpu.SMEM)
    anywhere = pl.BlockSpec(memory_space=pl.ANY)
    out_shape = jax.ShapeDtypeStruct((TOK, QHEADS * HEAD), jnp.bfloat16)
    first, worst, window = pl.pallas_call(
        functools.partial(kernel, outers),
        out_shape=(out_shape, jax.ShapeDtypeStruct((8, HEAD), jnp.float32),
                   jax.ShapeDtypeStruct((REACH, ROWS, HEAD), jnp.bfloat16)),
        in_specs=[smem, vmem, vmem, vmem],
        out_specs=(vmem, vmem, anywhere),
        scratch_shapes=[
            pltpu.VMEM((PARTS, ROWS, HEAD), jnp.bfloat16),
            pltpu.VMEM((QHEADS * TOK, 2 * HEAD), jnp.bfloat16),
            pltpu.VMEM((8, QHEADS * TOK), jnp.float32),
            pltpu.VMEM((HEAD + 16, QHEADS * TOK), jnp.float32),
            pltpu.SemaphoreType.DMA((2 * len(SENDS[0]),)),
            pltpu.SemaphoreType.DMA((2 * OWN,)),
            pltpu.SemaphoreType.DMA((REACH,)),
        ],
        compiler_params=pltpu.CompilerParams(
            collective_id=0, has_side_effects=True, vmem_limit_bytes=56 << 20),
        cost_estimate=pl.CostEstimate(
            flops=4 * 12 * QHEADS * TOK * TOK * HEAD, bytes_accessed=12 << 20,
            transcendentals=12 * QHEADS * TOK * TOK),
    )(doc_lengths, queries, keys, values)
    return pl.pallas_call(
        repair,
        out_shape=out_shape,
        in_specs=[smem, smem] + [anywhere] * 5,
        out_specs=anywhere,
        scratch_shapes=[
            pltpu.VMEM((TOK, QHEADS * HEAD), jnp.bfloat16),
            pltpu.VMEM((ROWS, HEAD), jnp.bfloat16),
            pltpu.VMEM((HEAD, TOK), jnp.bfloat16),
            pltpu.VMEM((TOK, HEAD), jnp.bfloat16),
            pltpu.VMEM((TOK, QHEADS * HEAD), jnp.bfloat16),
            pltpu.VMEM((8, QHEADS * TOK), jnp.float32),
            pltpu.VMEM((HEAD + 16, QHEADS * TOK), jnp.float32),
            pltpu.SemaphoreType.DMA((2, 4)),
        ],
        compiler_params=pltpu.CompilerParams(vmem_limit_bytes=56 << 20),
    )(worst, doc_lengths, queries, keys, values, window, first)


def solution(mesh):
    rows = P(("outer", "inner"), None)
    return jax.shard_map(
        functools.partial(per_device, mesh.shape["outer"]),
        mesh=mesh,
        in_specs=(rows, rows, rows, P()),
        out_specs=rows,
        check_vma=False,
    )
```
